256 devices in a mesh: wide: 16 (over z_lo, y), narrow: 16 (over x, z_hi, core).
Axes of the slice: x: 4, y: 4, z: 8 (z_hi: 2, z_lo: 4; z = z_hi * 4 + z_lo), core: 2. Of those that a mesh axis runs over, the one named last changes fastest.
Arguments:
- frame_queries: bfloat16 [65536, 1536], P(('wide', 'narrow')), may hold values from -8 to 8
- frame_keys: bfloat16 [65536, 1536], P(('wide', 'narrow')), may hold values from -8 to 8
- frame_values: bfloat16 [65536, 1536], P(('wide', 'narrow')), may hold values from -6 to 6
- short_head_offsets: int32 [24], replicated, may hold values from 0 to 1
- middle_head_offsets: int32 [24], replicated, may hold values from 0 to 31
- global_head_offsets: int32 [24], replicated, may hold values from 0 to 127
- w_out: bfloat16 [1536, 1536], replicated, may hold values from -1.25 to 1.25
Outputs:
- layer_out: float32 [65536, 1536], P(('wide', 'narrow'))
The draws below stay inside these ranges and needn't reach their ends.
All inputs are finite; a program needn't handle non-finite values.
Results may differ from the reference program's by a relative error of at most 0.0036.
Values may be sent and summed in bfloat16 or wider, within the bound.
A program may use at most 64 MiB of HBM per device.

```python
import math
import jax
import jax.numpy as jnp
from jax import lax

HEAD_TOTAL = 24
HEAD_SIZE = 64
KEPT_ROWS = 512
WIDTH = 1536
FRAMES = 65536
SHORT_DILATION = 2
MIDDLE_DILATION = 32
GLOBAL_DILATION = 128


def draw_frame_queries(key, part):
    key = jax.random.fold_in(key, 1)
    return jnp.clip(1.2 * jax.random.normal(key, (FRAMES, WIDTH), jnp.float32), -8.0, 8.0).astype(jnp.bfloat16)


def draw_frame_keys(key, part):
    key = jax.random.fold_in(key, 2)
    return jnp.clip(1.2 * jax.random.normal(key, (FRAMES, WIDTH), jnp.float32), -8.0, 8.0).astype(jnp.bfloat16)


def touch_ends(drawn, key, least, high):
    dims = drawn.shape
    spot = [jax.random.randint(jax.random.fold_in(key, axis), (), 0, dims[axis]) for axis in range(len(dims))]
    drawn = drawn.at[tuple(spot)].set(least)
    longest = dims.index(max(dims))
    spot[longest] = (spot[longest] + 1) % dims[longest]
    return drawn.at[tuple(spot)].set(high)


def levels(key, dims, shards, smallest, largest):
    gain, own = 1.0, jax.random.fold_in(key, 6)
    for axis_at, parts in shards:
        draws = jnp.exp(jax.random.uniform(jax.random.fold_in(own, axis_at), (parts,), jnp.float32, smallest / len(shards), largest / len(shards)))
        gain = gain * jnp.repeat(draws, dims[axis_at] // parts).reshape([-1 if axis == axis_at else 1 for axis in range(len(dims))])
    return gain


def scatter_about(rng, extent, width, bound, shards=(), kind=jnp.bfloat16):
    factor_of = levels(rng, extent, shards, -0.22, 0.18) if shards else 1.0
    values = jax.random.normal(rng, extent, jnp.float32) * width * factor_of
    return jnp.minimum(jnp.maximum(values, -bound), bound).astype(kind)


def setup_inputs(seed: int = 0) -> dict:
    key_list = jax.random.split(jax.random.key(seed), 8)
    return {
        "frame_queries": draw_frame_queries(jax.random.fold_in(key_list[7], 71), 0),
        "frame_keys": draw_frame_keys(jax.random.fold_in(key_list[7], 71), 0),
        "frame_values": scatter_about(key_list[2], (FRAMES, WIDTH), 1.0, 6.0, ((0, 256),)),
        "short_head_offsets": touch_ends(jax.random.randint(key_list[3], (HEAD_TOTAL,), 0, SHORT_DILATION), jax.random.fold_in(key_list[3], 1), 0, SHORT_DILATION - 1).astype(jnp.int32),
        "middle_head_offsets": touch_ends(jax.random.randint(key_list[4], (HEAD_TOTAL,), 0, MIDDLE_DILATION), jax.random.fold_in(key_list[4], 1), 0, MIDDLE_DILATION - 1).astype(jnp.int32),
        "global_head_offsets": touch_ends(jax.random.randint(key_list[5], (HEAD_TOTAL,), 0, GLOBAL_DILATION), jax.random.fold_in(key_list[5], 1), 0, GLOBAL_DILATION - 1).astype(jnp.int32),
        "w_out": scatter_about(key_list[6], (WIDTH, WIDTH), HEAD_TOTAL ** -0.5, 1.25),
    }


MASKED = -1e+30

def attend(sel_queries, sel_keys, sel_values):
    scores = jnp.einsum('qhd,khd->hqk', sel_queries.astype(jnp.float32), sel_keys.astype(jnp.float32)) * (1.0 / math.sqrt(HEAD_SIZE))
    row_peak = lax.optimization_barrier(jnp.max(scores, axis=2, keepdims=True))
    exp_scores = jnp.exp(scores - row_peak)
    totals = lax.optimization_barrier(jnp.sum(exp_scores, axis=2))
    prob_weights = exp_scores.astype(jnp.bfloat16)
    numerator = jnp.einsum('hqk,khd->qhd', prob_weights.astype(jnp.float32), sel_values.astype(jnp.float32))
    scope_out = numerator / jnp.transpose(totals)[:, :, None]
    scope_lse = jnp.transpose(row_peak[:, :, 0] + jnp.log(totals))
    return (scope_out, scope_lse)

def attend_triple(triple):
    return attend(triple[0], triple[1], triple[2])

def single_scope_attention(frame_queries, frame_keys, frame_values, dilation, offsets):
    seg_count = FRAMES // (KEPT_ROWS * dilation)
    picker = jnp.broadcast_to(offsets.astype(jnp.int32).reshape(1, 1, 1, HEAD_TOTAL, 1), (seg_count, KEPT_ROWS, 1, HEAD_TOTAL, HEAD_SIZE))

    def select_rows(source_arr):
        shaped = source_arr.reshape(seg_count, KEPT_ROWS, dilation, HEAD_TOTAL, HEAD_SIZE)
        return jnp.take_along_axis(shaped, picker, axis=2)[:, :, 0]
    picked = (select_rows(frame_queries), select_rows(frame_keys), select_rows(frame_values))
    results, spreads = lax.map(attend_triple, picked)
    covered = jnp.arange(dilation, dtype=jnp.int32)[:, None] == offsets.astype(jnp.int32)[None, :]
    lse_frames = jnp.where(covered[None, None], spreads[:, :, None, :], MASKED).reshape(FRAMES, HEAD_TOTAL)
    cover_frames = jnp.broadcast_to(covered[None, None], (seg_count, KEPT_ROWS, dilation, HEAD_TOTAL)).reshape(FRAMES, HEAD_TOTAL)
    return (results, lse_frames, cover_frames, covered)

def reference(frame_queries, frame_keys, frame_values, short_head_offsets, middle_head_offsets, global_head_offsets, w_out):
    scope_list = [single_scope_attention(frame_queries, frame_keys, frame_values, SHORT_DILATION, short_head_offsets), single_scope_attention(frame_queries, frame_keys, frame_values, MIDDLE_DILATION, middle_head_offsets), single_scope_attention(frame_queries, frame_keys, frame_values, GLOBAL_DILATION, global_head_offsets)]
    stacked_lse = jnp.stack([scope_item[1] for scope_item in scope_list])
    stacked_cover = jnp.stack([scope_item[2] for scope_item in scope_list])
    any_cover = jnp.any(stacked_cover, axis=0)
    top_lse = jnp.where(any_cover, lax.optimization_barrier(jnp.max(stacked_lse, axis=0)), 0.0)
    weights = jnp.where(stacked_cover, jnp.exp(stacked_lse - top_lse[None]), 0.0)
    denominator = jnp.where(any_cover, lax.optimization_barrier(jnp.sum(weights, axis=0)), 1.0)
    accumulated = jnp.zeros((FRAMES, HEAD_TOTAL, HEAD_SIZE), jnp.float32)
    for position in range(3):
        results = scope_list[position][0]
        covered = scope_list[position][3]
        full_out = jnp.where(covered[None, None, :, :, None], results[:, :, None], 0.0).reshape(FRAMES, HEAD_TOTAL, HEAD_SIZE)
        accumulated = accumulated + weights[position][:, :, None] * full_out
    merged = (accumulated / denominator[:, :, None]).astype(jnp.bfloat16).reshape(FRAMES, WIDTH)
    return jnp.dot(merged, w_out, preferred_element_type=jnp.float32)
```

```python
import math

import jax
import jax.numpy as jnp
from jax import lax
from jax.experimental import pallas as pl
from jax.experimental.pallas import tpu as pltpu
from jax.sharding import PartitionSpec as P

MESH = pl.DeviceIdType.MESH
F32 = jnp.float32
BF16 = jnp.bfloat16

LANES = 128
HEAD_DIM = 64
TILES = 12
GROUPS = 4
GROUP_TILES = TILES // GROUPS
X_CHIPS, Y_CHIPS, Z_CHIPS = 4, 4, 8
FRAMES = 256
SHORT_ROWS, MIDDLE_ROWS, GLOBAL_ROWS = 128, 8, 2
KEPT_ROWS = 512
PACKET = 32
SENDERS = 8
AHEAD = 3
X_TILE, MERGE_TILE, FINISH_TILE = 3, 5, 6
MASKED = -1e30

SIBLING, ACROSS, PASSED_ON, PACKETS, ALONG_Z, ALONG_X, RESULTS = range(7)


def first_head():
    return lax.broadcasted_iota(jnp.int32, (1, LANES), 1) < HEAD_DIM


def attend(query, key, value):
    rows = query.shape[0]
    first = first_head()
    low = first.astype(F32).astype(BF16)
    high = (1.0 - first.astype(F32)).astype(BF16)
    stacked = jnp.concatenate([query * low, query * high], axis=0)
    scores = lax.dot_general(
        stacked, key, (((1,), (1,)), ((), ())), preferred_element_type=F32
    ) * (1.0 / math.sqrt(HEAD_DIM))
    peak = jnp.max(scores, axis=1, keepdims=True)
    exps = jnp.exp(scores - peak)
    total = jnp.sum(exps, axis=1, keepdims=True)
    numerator = jnp.dot(exps.astype(BF16), value, preferred_element_type=F32)
    output = numerator / total
    spread = jnp.broadcast_to(peak + jnp.log(total), (2 * rows, LANES))
    return (
        jnp.where(first, output[:rows], output[rows:]),
        jnp.where(first, spread[:rows], spread[rows:]),
    )


def kernel(
    short_hbm, middle_hbm, global_hbm, q_hbm, k_hbm, v_hbm, w_hbm, o_ref, short_off, middle_off, global_off,
    q_in, k_in, v_in, w_in, plain, short_q, short_kv, short_out, packets, collected, role_q, gathered,
    role_out, results, merged, load_sem, send_sem, recv_sem,
):
    wide, narrow = lax.axis_index("wide"), lax.axis_index("narrow")
    x, y, c = narrow // 4, lax.rem(wide, 4), lax.rem(narrow, 2)
    z_hi, z_lo = lax.rem(narrow // 2, 2), wide // 4
    z = z_hi * 4 + z_lo
    me = y * 2 + c

    def device(dx=0, dy=0, dz=0, dc=0):
        to_z = lax.rem(z + dz, Z_CHIPS)
        return {
            "wide": lax.rem(to_z, 4) * 4 + lax.rem(y + dy, Y_CHIPS),
            "narrow": lax.rem(x + dx, X_CHIPS) * 4 + to_z // 4 * 2 + lax.rem(c + dc, 2),
        }

    def send(source, target, kind, number, to):
        return pltpu.make_async_remote_copy(
            src_ref=source, dst_ref=target, send_sem=send_sem.at[kind, number], recv_sem=recv_sem.at[kind, number],
            device_id=to, device_id_type=MESH,
        )

    def to_sibling(i):
        return send(short_kv.at[i, 0], short_kv.at[i, 1], SIBLING, i, device(dc=1))

    def across(i):
        return send(short_kv.at[i, 0], short_kv.at[i, 2], ACROSS, i, device(dz=4))

    def pass_on(i):
        return send(short_kv.at[i, 2], short_kv.at[i, 3], PASSED_ON, i, device(dc=1))

    group = [(dy, dc) for dy in range(Y_CHIPS) for dc in range(2) if dy or dc]

    def packet_to(number):
        dy, dc = group[number]
        to_y = lax.rem(y + dy, Y_CHIPS)
        return send(
            packets.at[pl.ds(to_y * GROUP_TILES, GROUP_TILES)], collected.at[me], PACKETS, number, device(dy=dy, dc=dc)
        )

    def result_to(number):
        dy, dc = group[number]
        sender = lax.rem(y + dy, Y_CHIPS) * 2 + lax.rem(c + dc, 2)
        return send(
            role_out.at[sender], results.at[c, pl.ds(y * GROUP_TILES, GROUP_TILES)], RESULTS, number, device(dy=dy, dc=dc)
        )

    def middle_along_z():
        part = gathered.at[x, :, :, pl.ds(z_hi * 64, 64)]
        return send(part, part, ALONG_Z, 4, device(dz=4))

    def global_along_z(dz):
        part = gathered.at[x, :, :, pl.ds(z * 16, 16)]
        return send(part, part, ALONG_Z, dz, device(dz=dz))

    def along_x(dx):
        return send(gathered.at[x], gathered.at[x], ALONG_X, dx, device(dx=dx))

    barrier = pltpu.get_barrier_semaphore()
    partners = [dict(dy=dy, dc=dc) for dy, dc in group]
    partners += [dict(dx=dx) for dx in range(1, X_CHIPS)]
    partners += [dict(dz=dz) for dz in range(1, Z_CHIPS)]
    for partner in partners:
        pl.semaphore_signal(barrier, inc=1, device_id=device(**partner), device_id_type=MESH)

    loads = [
        pltpu.make_async_copy(source, target, load_sem.at[number])
        for number, (source, target) in enumerate((
            (short_hbm, short_off), (middle_hbm, middle_off), (global_hbm, global_off),
            (k_hbm, k_in), (v_hbm, v_in), (q_hbm, q_in), (w_hbm, w_in),
        ))
    ]
    for load in loads:
        load.start()

    first = first_head()

    def offsets(ref, i):
        return jnp.where(first, ref[2 * i], ref[2 * i + 1])

    def select_short(source, number, i):
        lanes = pl.ds(pl.multiple_of(i * LANES, LANES), LANES)
        plain[number] = source[:, lanes].astype(F32)
        even = plain[number, pl.ds(0, SHORT_ROWS, stride=2), :]
        odd = plain[number, pl.ds(1, SHORT_ROWS, stride=2), :]
        return jnp.where(offsets(short_off, i) == 0, even, odd).astype(BF16)

    for load in loads[:5]:
        load.wait()

    @pl.loop(0, TILES)
    def _(i):
        short_kv[i, 0, 0] = select_short(k_in, 0, i)
        short_kv[i, 0, 1] = select_short(v_in, 1, i)

    pl.semaphore_wait(barrier, len(partners))

    @pl.loop(0, AHEAD)
    def _(i):
        across(i).start()

    loads[5].wait()

    @pl.loop(0, TILES)
    def _(i):
        lanes = pl.ds(pl.multiple_of(i * LANES, LANES), LANES)
        to_sibling(i).start()
        middle_at = offsets(middle_off, i)
        global_at = offsets(global_off, i)
        frame = lax.broadcasted_iota(jnp.int32, (FRAMES, LANES), 0)
        in_middle = lax.rem(frame, 32) == middle_at
        in_global = lax.rem(frame, 128) == global_at
        eight = lax.broadcasted_iota(jnp.int32, (8, LANES), 0)
        rows = []
        last = jnp.zeros((8, LANES), F32)
        for number, source in enumerate((q_in, k_in, v_in)):
            values = source[:, lanes].astype(F32)
            rows.append(jnp.sum(jnp.where(in_middle, values, 0.0).reshape(MIDDLE_ROWS, 32, LANES), axis=1))
            global_rows = jnp.sum(jnp.where(in_global, values, 0.0).reshape(GLOBAL_ROWS, 128, LANES), axis=1)
            for row in range(GLOBAL_ROWS):
                last = jnp.where(eight == 2 * number + row, global_rows[row : row + 1], last)
        packets[i] = jnp.concatenate([*rows, last], axis=0).astype(BF16)

    for number in range(len(group)):
        packet_to(number).start()
    collected[me] = packets[pl.ds(y * GROUP_TILES, GROUP_TILES)]

    @pl.loop(0, TILES)
    def _(i):
        short_q[i] = select_short(q_in, 2, i)

    o_ref[...] = jnp.zeros_like(o_ref)

    for number in range(len(group)):
        packet_to(number).wait_recv()

    def pick(row_total, place):
        row = lax.broadcasted_iota(jnp.int32, (row_total, SENDERS * PACKET), 0)
        column = lax.broadcasted_iota(jnp.int32, (row_total, SENDERS * PACKET), 1)
        return jnp.where(column == place(row), 1.0, 0.0).astype(BF16)

    def take(one_hot, tile):
        rows = collected[:, tile].reshape(SENDERS * PACKET, LANES)
        return jnp.dot(one_hot, rows, preferred_element_type=F32).astype(BF16)

    @pl.when(c == 0)
    def _():
        def place(first_row):
            return lambda row: row // 8 * PACKET + first_row + lax.rem(row, 8)

        picks = [pick(64, place(first_row)) for first_row in (0, 8, 16)]
        for tile in range(GROUP_TILES):
            role_q[tile] = take(picks[0], tile)
            for part in range(2):
                gathered[x, tile, part, pl.ds(z_hi * 64, 64), :] = take(picks[1 + part], tile)
        middle_along_z().start()

    @pl.when(c == 1)
    def _():
        def place_query(row):
            within = lax.rem(row, 8)
            return jnp.where(within < GLOBAL_ROWS, row // 8 * PACKET + 24 + within, -1)

        def place(first_row):
            return lambda row: row // 2 * PACKET + first_row + lax.rem(row, 2)

        picks = [pick(64, place_query)] + [pick(16, place(first_row)) for first_row in (26, 28)]
        for tile in range(GROUP_TILES):
            role_q[tile] = take(picks[0], tile)
            for part in range(2):
                gathered[x, tile, part, pl.ds(z * 16, 16), :] = take(picks[1 + part], tile)
        for dz in range(1, Z_CHIPS):
            global_along_z(dz).start()

    @pl.loop(AHEAD, TILES)
    def _(i):
        across(i).start()

    def short_scope(i):
        across(i).wait_recv()
        pass_on(i).start()
        to_sibling(i).wait_recv()
        pass_on(i).wait_recv()
        output, spread = attend(
            short_q[i],
            short_kv[i, :, 0].reshape(KEPT_ROWS, LANES),
            short_kv[i, :, 1].reshape(KEPT_ROWS, LANES),
        )
        short_out[i, 0] = output
        short_out[i, 1] = spread

    def finish(i):
        short_at, middle_at, global_at = (offsets(ref, i) for ref in (short_off, middle_off, global_off))
        for parity in range(2):
            shape = (SHORT_ROWS, LANES)
            row = lax.broadcasted_iota(jnp.int32, shape, 0)
            covers = (
                jnp.broadcast_to(short_at == parity, shape),
                2 * lax.rem(row, 16) + parity == middle_at,
                2 * lax.rem(row, 64) + parity == global_at,
            )

            def spread_out(value, count):
                return jnp.broadcast_to(
                    value[:count].reshape(count, 1, LANES), (count, SHORT_ROWS // count, LANES)
                ).reshape(shape)

            outs = (
                short_out[i, 0],
                spread_out(results[0, i, 0], MIDDLE_ROWS),
                spread_out(results[1, i, 0], GLOBAL_ROWS),
            )
            spreads = (
                short_out[i, 1],
                spread_out(results[0, i, 1], MIDDLE_ROWS),
                spread_out(results[1, i, 1], GLOBAL_ROWS),
            )
            masked = [jnp.where(cover, value, MASKED) for cover, value in zip(covers, spreads)]
            top = jnp.maximum(jnp.maximum(masked[0], masked[1]), masked[2])
            weights = [jnp.where(cover, jnp.exp(value - top), 0.0) for cover, value in zip(covers, masked)]
            denominator = weights[0] + weights[1] + weights[2]
            denominator = jnp.where(denominator == 0.0, 1.0, denominator)
            total = weights[0] * outs[0] + weights[1] * outs[1] + weights[2] * outs[2]
            merged[pl.ds(parity, SHORT_ROWS, stride=2), :] = total / denominator
        rows = merged[...].astype(BF16)
        depth = pl.ds(pl.multiple_of(i * LANES, LANES), LANES)
        for part in range(3):
            columns = pl.ds(part * 512, 512)
            o_ref[:, columns] += jnp.dot(rows, w_in[depth, columns], preferred_element_type=F32)

    @pl.loop(0, TILES)
    def _(i):
        @pl.when(i == X_TILE)
        def _():
            @pl.when(c == 0)
            def _():
                middle_along_z().wait_recv()

            @pl.when(c == 1)
            def _():
                for dz in range(1, Z_CHIPS):
                    global_along_z(dz).wait_recv()

            for dx in range(1, X_CHIPS):
                along_x(dx).start()

        @pl.when(i == MERGE_TILE)
        def _():
            for dx in range(1, X_CHIPS):
                along_x(dx).wait_recv()

            for tile in range(GROUP_TILES):
                output, spread = attend(
                    role_q[tile],
                    gathered[:, tile, 0].reshape(KEPT_ROWS, LANES),
                    gathered[:, tile, 1].reshape(KEPT_ROWS, LANES),
                )
                role_out[:, tile, 0] = output.reshape(SENDERS, 8, LANES)
                role_out[:, tile, 1] = spread.reshape(SENDERS, 8, LANES)
            for number in range(len(group)):
                result_to(number).start()
            results[c, pl.ds(y * GROUP_TILES, GROUP_TILES)] = role_out[me]

        short_scope(i)

        @pl.when(i == FINISH_TILE)
        def _():
            for number in range(len(group)):
                result_to(number).wait_recv()
            loads[6].wait()

        @pl.when(i >= FINISH_TILE)
        def _():
            @pl.loop(jnp.where(i == FINISH_TILE, 0, i), i + 1)
            def _(tile):
                finish(tile)

    @pl.loop(0, TILES)
    def _(i):
        to_sibling(i).wait_send()
        across(i).wait_send()
        pass_on(i).wait_send()

    for number in range(len(group)):
        packet_to(number).wait_send()
        result_to(number).wait_send()
    for dx in range(1, X_CHIPS):
        along_x(dx).wait_send()

    @pl.when(c == 0)
    def _():
        middle_along_z().wait_send()

    @pl.when(c == 1)
    def _():
        for dz in range(1, Z_CHIPS):
            global_along_z(dz).wait_send()


def per_device(queries, keys, values, short_offsets, middle_offsets, global_offsets, w_out):
    frames, width = queries.shape
    heads = short_offsets.shape
    return pl.pallas_call(
        kernel,
        out_shape=jax.ShapeDtypeStruct((frames, width), F32),
        in_specs=[pl.BlockSpec(memory_space=pltpu.HBM)] * 7,
        out_specs=pl.BlockSpec(memory_space=pltpu.VMEM),
        scratch_shapes=[
            pltpu.SMEM(heads, jnp.int32),
            pltpu.SMEM(heads, jnp.int32),
            pltpu.SMEM(heads, jnp.int32),
            pltpu.VMEM((frames, width), BF16),
            pltpu.VMEM((frames, width), BF16),
            pltpu.VMEM((frames, width), BF16),
            pltpu.VMEM((width, width), BF16),
            pltpu.VMEM((3, frames, LANES), F32),
            pltpu.VMEM((TILES, SHORT_ROWS, LANES), BF16),
            pltpu.VMEM((TILES, 4, 2, SHORT_ROWS, LANES), BF16),
            pltpu.VMEM((TILES, 2, SHORT_ROWS, LANES), F32),
            pltpu.VMEM((TILES, PACKET, LANES), BF16),
            pltpu.VMEM((SENDERS, GROUP_TILES, PACKET, LANES), BF16),
            pltpu.VMEM((GROUP_TILES, 64, LANES), BF16),
            pltpu.VMEM((X_CHIPS, GROUP_TILES, 2, 128, LANES), BF16),
            pltpu.VMEM((SENDERS, GROUP_TILES, 2, 8, LANES), F32),
            pltpu.VMEM((2, TILES, 2, 8, LANES), F32),
            pltpu.VMEM((frames, LANES), F32),
            pltpu.SemaphoreType.DMA((7,)),
            pltpu.SemaphoreType.DMA((7, TILES)),
            pltpu.SemaphoreType.DMA((7, TILES)),
        ],
        compiler_params=pltpu.CompilerParams(
            collective_id=0, has_side_effects=True, vmem_limit_bytes=60 * 1024 * 1024
        ),
        name="dilated_attention",
    )(short_offsets, middle_offsets, global_offsets, queries, keys, values, w_out)


def solution(mesh):
    placed = (
        P(("wide", "narrow"), None),
        P(("wide", "narrow"), None),
        P(("wide", "narrow"), None),
        P(),
        P(),
        P(),
        P(),
    )
    return jax.shard_map(
        per_device,
        mesh=mesh,
        in_specs=placed,
        out_specs=P(("wide", "narrow"), None),
        check_vma=False,
    )
```

```python
import math

import jax
import jax.numpy as jnp
from jax import lax
from jax.experimental import pallas as pl
from jax.experimental.pallas import tpu as pltpu
from jax.sharding import PartitionSpec as P

MESH = pl.DeviceIdType.MESH
F32 = jnp.float32
BF16 = jnp.bfloat16

LANES = 128
HEAD_DIM = 64
TILES = 12
X_CHIPS, Y_CHIPS, Z_CHIPS = 4, 4, 8
CHIPS = X_CHIPS * Y_CHIPS
PLANE = 2 * CHIPS
FRAMES = 256
SHORT_ROWS, MIDDLE_ROWS, GLOBAL_ROWS = 128, 8, 2
KEPT_ROWS = 512
MIDDLE_PACKET = 32
GLOBAL_PACKET = 16
BLOCK = 8
BLOCKS = PLANE // BLOCK
GLOBAL_SHIFT = 4
AHEAD = 6
FINISH_TILE = 6
PROJECTED = (0, FINISH_TILE, 9, 11, 12)
MASKED = -1e30

SIBLING, ACROSS, PASSED_ON, ALONG_Z = range(4)


def first_head():
    return lax.broadcasted_iota(jnp.int32, (1, LANES), 1) < HEAD_DIM


def attend(query, key, value):
    rows = query.shape[0]
    first = first_head()
    low = first.astype(F32).astype(BF16)
    high = (1.0 - first.astype(F32)).astype(BF16)
    stacked = jnp.concatenate([query * low, query * high], axis=0)
    scores = lax.dot_general(
        stacked, key, (((1,), (1,)), ((), ())), preferred_element_type=F32
    ) * (1.0 / math.sqrt(HEAD_DIM))
    peak = jnp.max(scores, axis=1, keepdims=True)
    exps = jnp.exp(scores - peak)
    total = jnp.sum(exps, axis=1, keepdims=True)
    numerator = jnp.dot(exps.astype(BF16), value, preferred_element_type=F32)
    output = numerator / total
    spread = jnp.broadcast_to(peak + jnp.log(total), (2 * rows, LANES))
    return (
        jnp.where(first, output[:rows], output[rows:]),
        jnp.where(first, spread[:rows], spread[rows:]),
    )


def kernel(
    short_hbm, middle_hbm, global_hbm, q_hbm, k_hbm, v_hbm, w_hbm, o_ref, short_off, middle_off, global_off,
    q_in, k_in, v_in, w_in, plain, short_q, short_kv, short_out, middle_packets, global_packets, middle_in, global_in,
    role_q, gathered, role_out, results, merged, merged_rows, load_sem, send_sem, recv_sem, packet_send, packet_recv,
    result_send, result_recv, go_sem, row_sem,
):
    wide, narrow = lax.axis_index("wide"), lax.axis_index("narrow")
    x, y, c = narrow // 4, lax.rem(wide, 4), lax.rem(narrow, 2)
    z = lax.rem(narrow // 2, 2) * 4 + wide // 4
    z_hi = z // 4
    chip = x * 4 + y
    me = chip * 2 + c
    early = lax.rem(z // 2, 2) == 1

    def at(plane_place, to_z):
        to_chip = plane_place // 2
        return {
            "wide": lax.rem(to_z, 4) * 4 + lax.rem(to_chip, 4),
            "narrow": to_chip // 4 * 4 + to_z // 4 * 2 + lax.rem(plane_place, 2),
        }

    sibling = at(chip * 2 + 1 - c, z)

    def along_z(dz):
        return at(me, lax.rem(z + dz, Z_CHIPS))

    def send(source, target, send_to, recv_to, to):
        return pltpu.make_async_remote_copy(
            src_ref=source, dst_ref=target, send_sem=send_to, recv_sem=recv_to,
            device_id=to, device_id_type=MESH,
        )

    def to_sibling(i):
        return send(short_kv.at[i, 0], short_kv.at[i, 1], send_sem.at[SIBLING, i], recv_sem.at[SIBLING, i], sibling)

    def across(i):
        return send(short_kv.at[i, 0], short_kv.at[i, 2], send_sem.at[ACROSS, i], recv_sem.at[ACROSS, i], along_z(4))

    def pass_on(i):
        return send(short_kv.at[i, 2], short_kv.at[i, 3], send_sem.at[PASSED_ON, i], recv_sem.at[PASSED_ON, i], sibling)

    def worker(scope, tile):
        if scope == 0:
            return tile * 2
        return lax.rem(tile + GLOBAL_SHIFT, CHIPS) * 2 + 1

    own_tile = jnp.where(c == 0, chip, lax.rem(chip + CHIPS - GLOBAL_SHIFT, CHIPS))
    works = own_tile < TILES
    sibling_works = jnp.where(c == 0, chip >= GLOBAL_SHIFT, chip < TILES)

    def packet_to(scope, tile):
        source, target = ((middle_packets, middle_in), (global_packets, global_in))[scope]
        return send(
            source.at[tile], target.at[me], packet_send.at[scope, tile], packet_recv.at[me], at(worker(scope, tile), z)
        )

    def packet_from(scope, place):
        source, target = ((middle_packets, middle_in), (global_packets, global_in))[scope]
        return send(source.at[0], target.at[place], packet_send.at[scope, 0], packet_recv.at[place], at(place, z))

    def result_to(place):
        return send(
            role_out.at[place], results.at[c, own_tile], result_send.at[place], result_recv.at[c, own_tile], at(place, z)
        )

    def result_from(scope, tile):
        return send(
            role_out.at[0], results.at[scope, tile], result_send.at[0], result_recv.at[scope, tile],
            at(worker(scope, tile), z),
        )

    def middle_across():
        part = gathered.at[pl.ds(z_hi * 4, 4)]
        return send(part, part, send_sem.at[ALONG_Z, 4], recv_sem.at[ALONG_Z, 4], along_z(4))

    def global_to(dz):
        part = gathered.at[z]
        return send(part, part, send_sem.at[ALONG_Z, dz], recv_sem.at[ALONG_Z, dz], along_z(dz))

    barrier = pltpu.get_barrier_semaphore()

    def greet(to):
        pl.semaphore_signal(barrier, inc=1, device_id=to, device_id_type=MESH)

    greet(along_z(4))
    column = [
        at((x * 4 + lax.rem(y + dy, Y_CHIPS)) * 2 + lax.rem(c + dc, 2), z)
        for dy in range(Y_CHIPS) for dc in range(2) if dy or dc
    ]
    row = [at((lax.rem(x + dx, X_CHIPS) * 4 + y) * 2 + c, z) for dx in range(1, X_CHIPS)]
    for to in column + row:
        greet(to)

    @pl.when(c == 1)
    def _():
        for dz in (1, 2, 3, 5, 6, 7):
            greet(along_z(dz))

    loads = [
        pltpu.make_async_copy(source, target, load_sem.at[number])
        for number, (source, target) in enumerate((
            (short_hbm, short_off), (middle_hbm, middle_off), (global_hbm, global_off),
            (k_hbm, k_in), (v_hbm, v_in), (q_hbm, q_in), (w_hbm, w_in),
        ))
    ]
    for load in loads[:5]:
        load.start()

    first = first_head()

    def offsets(ref, i):
        return jnp.where(first, ref[2 * i], ref[2 * i + 1])

    def select_short(source, number, i):
        lanes = pl.ds(pl.multiple_of(i * LANES, LANES), LANES)
        plain[number] = source[:, lanes].astype(F32)
        even = plain[number, pl.ds(0, SHORT_ROWS, stride=2), :]
        odd = plain[number, pl.ds(1, SHORT_ROWS, stride=2), :]
        return jnp.where(offsets(short_off, i) == 0, even, odd).astype(BF16)

    for load in loads[:5]:
        load.wait()
    loads[5].start()

    @pl.loop(0, TILES)
    def _(i):
        short_kv[i, 0, 0] = select_short(k_in, 0, i)
        short_kv[i, 0, 1] = select_short(v_in, 1, i)

    pl.semaphore_wait(barrier, 1 + len(column) + len(row) + 6 * c)

    for to in row:
        pl.semaphore_signal(row_sem, inc=1, device_id=to, device_id_type=MESH)

    @pl.loop(0, jnp.where(early, AHEAD, 0))
    def _(i):
        across(i).start()

    loads[5].wait()

    @pl.loop(0, TILES)
    def _(i):
        lanes = pl.ds(pl.multiple_of(i * LANES, LANES), LANES)
        middle_at = offsets(middle_off, i)
        global_at = offsets(global_off, i)
        frame = lax.broadcasted_iota(jnp.int32, (FRAMES, LANES), 0)
        in_middle = lax.rem(frame, 32) == middle_at
        in_global = lax.rem(frame, 128) == global_at
        eight = lax.broadcasted_iota(jnp.int32, (8, LANES), 0)
        rows = []
        last = jnp.zeros((8, LANES), F32)
        for number, source in enumerate((q_in, k_in, v_in)):
            values = source[:, lanes].astype(F32)
            rows.append(jnp.sum(jnp.where(in_middle, values, 0.0).reshape(MIDDLE_ROWS, 32, LANES), axis=1))
            global_rows = jnp.sum(jnp.where(in_global, values, 0.0).reshape(GLOBAL_ROWS, 128, LANES), axis=1)
            for row in range(GLOBAL_ROWS):
                last = jnp.where(eight == 2 * number + row, global_rows[row : row + 1], last)
        middle_packets[i] = jnp.concatenate([*rows, jnp.zeros((8, LANES), F32)], axis=0).astype(BF16)
        global_packets[i] = jnp.concatenate([last, jnp.zeros((8, LANES), F32)], axis=0).astype(BF16)

    pl.semaphore_wait(row_sem, len(row))

    @pl.loop(0, TILES)
    def _(step):
        tile = lax.rem(step + me, TILES)
        for scope, (source, target) in enumerate(((middle_packets, middle_in), (global_packets, global_in))):
            @pl.when(worker(scope, tile) != me)
            def _():
                packet_to(scope, tile).start()

            @pl.when(worker(scope, tile) == me)
            def _():
                target[me] = source[tile]

    loads[6].start()

    @pl.loop(0, TILES)
    def _(i):
        to_sibling(i).start()
        short_q[i] = select_short(q_in, 2, i)

    def pick(shape, place):
        row = lax.broadcasted_iota(jnp.int32, shape, 0)
        column = lax.broadcasted_iota(jnp.int32, shape, 1)
        return jnp.where(column == place(row), 1.0, 0.0).astype(BF16)

    def take(one_hot, rows):
        return jnp.dot(one_hot, rows, preferred_element_type=F32).astype(BF16)

    @pl.when(works & (c == 0))
    def _():
        @pl.loop(1, PLANE)
        def _(step):
            packet_from(0, lax.rem(me + step, PLANE)).wait_recv()

        def place(first_row):
            return lambda row: row // 8 * MIDDLE_PACKET + first_row + lax.rem(row, 8)

        picks = [pick((64, BLOCK * MIDDLE_PACKET), place(first_row)) for first_row in (0, 8, 16)]

        @pl.loop(0, BLOCKS)
        def _(block):
            rows = middle_in[pl.ds(block * BLOCK, BLOCK)].reshape(BLOCK * MIDDLE_PACKET, LANES)
            role_q[block] = take(picks[0], rows)
            for part in range(2):
                gathered[z_hi * 4 + block, part] = take(picks[1 + part], rows)

        middle_across().start()

    @pl.when(works & (c == 1))
    def _():
        @pl.loop(1, PLANE)
        def _(step):
            packet_from(1, lax.rem(me + step, PLANE)).wait_recv()

        def place_query(row):
            within = lax.rem(row, 8)
            return jnp.where(within < GLOBAL_ROWS, row // 8 * GLOBAL_PACKET + within, -1)

        def place(first_row):
            return lambda row: row // 2 * GLOBAL_PACKET + first_row + lax.rem(row, 2)

        rows = global_in[...].reshape(PLANE * GLOBAL_PACKET, LANES)
        for part in range(2):
            gathered[z, part] = take(pick((64, PLANE * GLOBAL_PACKET), place(2 + 2 * part)), rows)
        for dz in range(1, Z_CHIPS):
            global_to(dz).start()
        query_pick = pick((64, BLOCK * GLOBAL_PACKET), place_query)

        @pl.loop(0, BLOCKS)
        def _(block):
            role_q[block] = take(
                query_pick, global_in[pl.ds(block * BLOCK, BLOCK)].reshape(BLOCK * GLOBAL_PACKET, LANES)
            )

    @pl.loop(jnp.where(early, TILES, 0), TILES)
    def _(i):
        across(i).start()

    def wait_along_z():
        @pl.when(works & (c == 0))
        def _():
            middle_across().wait_recv()

        @pl.when(works & (c == 1))
        def _():
            for dz in range(1, Z_CHIPS):
                global_to(dz).wait_recv()

        @pl.when(early & works & ~sibling_works)
        def _():
            pl.semaphore_signal(go_sem, inc=1, device_id=sibling, device_id_type=MESH)

        @pl.when(early & ~works)
        def _():
            pl.semaphore_wait(go_sem, 1)

        @pl.loop(jnp.where(early, AHEAD, TILES), TILES)
        def _(i):
            across(i).start()

    def work():
        key = gathered[:, 0].reshape(KEPT_ROWS, LANES)
        value = gathered[:, 1].reshape(KEPT_ROWS, LANES)

        @pl.loop(0, BLOCKS)
        def _(block):
            output, spread = attend(role_q[block], key, value)
            places = pl.ds(block * BLOCK, BLOCK)
            role_out[places, 0] = output.reshape(BLOCK, 8, LANES)
            role_out[places, 1] = spread.reshape(BLOCK, 8, LANES)

        @pl.loop(1, PLANE)
        def _(step):
            result_to(lax.rem(me + step, PLANE)).start()

        results[c, own_tile] = role_out[me]

    def short_scope(i):
        to_sibling(i).wait_recv()
        pass_on(i).wait_recv()
        output, spread = attend(
            short_q[i],
            short_kv[i, :, 0].reshape(KEPT_ROWS, LANES),
            short_kv[i, :, 1].reshape(KEPT_ROWS, LANES),
        )
        short_out[i, 0] = output
        short_out[i, 1] = spread

    def finish(i):
        short_at, middle_at, global_at = (offsets(ref, i) for ref in (short_off, middle_off, global_off))
        for parity in range(2):
            shape = (SHORT_ROWS, LANES)
            row = lax.broadcasted_iota(jnp.int32, shape, 0)
            covers = (
                jnp.broadcast_to(short_at == parity, shape),
                2 * lax.rem(row, 16) + parity == middle_at,
                2 * lax.rem(row, 64) + parity == global_at,
            )

            def spread_out(value, count):
                return jnp.broadcast_to(
                    value[:count].reshape(count, 1, LANES), (count, SHORT_ROWS // count, LANES)
                ).reshape(shape)

            outs = (
                short_out[i, 0],
                spread_out(results[0, i, 0], MIDDLE_ROWS),
                spread_out(results[1, i, 0], GLOBAL_ROWS),
            )
            spreads = (
                short_out[i, 1],
                spread_out(results[0, i, 1], MIDDLE_ROWS),
                spread_out(results[1, i, 1], GLOBAL_ROWS),
            )
            masked = [jnp.where(cover, value, MASKED) for cover, value in zip(covers, spreads)]
            top = jnp.maximum(jnp.maximum(masked[0], masked[1]), masked[2])
            weights = [jnp.where(cover, jnp.exp(value - top), 0.0) for cover, value in zip(covers, masked)]
            denominator = weights[0] + weights[1] + weights[2]
            denominator = jnp.where(denominator == 0.0, 1.0, denominator)
            total = weights[0] * outs[0] + weights[1] * outs[1] + weights[2] * outs[2]
            merged[pl.ds(parity, SHORT_ROWS, stride=2), :] = total / denominator
        merged_rows[:, pl.ds(pl.multiple_of(i * LANES, LANES), LANES)] = merged[...].astype(BF16)

    def project(first_tile, end_tile):
        depth = pl.ds(first_tile * LANES, (end_tile - first_tile) * LANES)
        for part in range(6):
            columns = pl.ds(part * 256, 256)
            product = jnp.dot(merged_rows[:, depth], w_in[depth, columns], preferred_element_type=F32)
            if first_tile:
                product += o_ref[:, columns]
            o_ref[:, columns] = product

    def wait_results():
        @pl.loop(0, TILES)
        def _(tile):
            for scope in range(2):
                @pl.when(worker(scope, tile) != me)
                def _():
                    result_from(scope, tile).wait_recv()

    def sent(i):
        to_sibling(i).wait_send()
        across(i).wait_send()
        pass_on(i).wait_send()

    def sent_rows():
        @pl.loop(0, TILES)
        def _(i):
            for scope in range(2):
                @pl.when(worker(scope, i) != me)
                def _():
                    packet_to(scope, i).wait_send()

        @pl.when(works)
        def _():
            @pl.loop(1, PLANE)
            def _(step):
                result_to(lax.rem(me + step, PLANE)).wait_send()

            @pl.when(c == 0)
            def _():
                middle_across().wait_send()

            @pl.when(c == 1)
            def _():
                for dz in range(1, Z_CHIPS):
                    global_to(dz).wait_send()

    merge_tile = jnp.where(early, AHEAD, 0)

    @pl.loop(0, TILES + 1)
    def _(i):
        @pl.when(i == merge_tile)
        def _():
            wait_along_z()

        @pl.when((i == merge_tile) & works)
        def _():
            work()

        @pl.when(i < TILES)
        def _():
            across(i).wait_recv()
            pass_on(i).start()

        @pl.when(i > 0)
        def _():
            short_scope(i - 1)

        @pl.when(i == FINISH_TILE)
        def _():
            wait_results()
            loads[6].wait()

        @pl.when(i >= FINISH_TILE)
        def _():
            @pl.loop(jnp.where(i == FINISH_TILE, 0, i - 1), i)
            def _(tile):
                finish(tile)

        for first_tile, end_tile in zip(PROJECTED, PROJECTED[1:]):
            @pl.when(i == end_tile)
            def _():
                project(first_tile, end_tile)

        @pl.when(i > 1)
        def _():
            sent(i - 2)

        @pl.when(i == 9)
        def _():
            sent_rows()

    sent(TILES - 1)


def per_device(queries, keys, values, short_offsets, middle_offsets, global_offsets, w_out):
    frames, width = queries.shape
    heads = short_offsets.shape
    return pl.pallas_call(
        kernel,
        out_shape=pltpu.VMEM((frames, width), F32),
        in_specs=[pl.BlockSpec(memory_space=pltpu.HBM)] * 7,
        out_specs=pl.BlockSpec(memory_space=pltpu.VMEM),
        scratch_shapes=[
            pltpu.SMEM(heads, jnp.int32),
            pltpu.SMEM(heads, jnp.int32),
            pltpu.SMEM(heads, jnp.int32),
            pltpu.VMEM((frames, width), BF16),
            pltpu.VMEM((frames, width), BF16),
            pltpu.VMEM((frames, width), BF16),
            pltpu.VMEM((width, width), BF16),
            pltpu.VMEM((3, frames, LANES), F32),
            pltpu.VMEM((TILES, SHORT_ROWS, LANES), BF16),
            pltpu.VMEM((TILES, 4, 2, SHORT_ROWS, LANES), BF16),
            pltpu.VMEM((TILES, 2, SHORT_ROWS, LANES), F32),
            pltpu.VMEM((TILES, MIDDLE_PACKET, LANES), BF16),
            pltpu.VMEM((TILES, GLOBAL_PACKET, LANES), BF16),
            pltpu.VMEM((PLANE, MIDDLE_PACKET, LANES), BF16),
            pltpu.VMEM((PLANE, GLOBAL_PACKET, LANES), BF16),
            pltpu.VMEM((BLOCKS, 64, LANES), BF16),
            pltpu.VMEM((8, 2, 64, LANES), BF16),
            pltpu.VMEM((PLANE, 2, 8, LANES), F32),
            pltpu.VMEM((2, TILES, 2, 8, LANES), F32),
            pltpu.VMEM((frames, LANES), F32),
            pltpu.VMEM((frames, width), BF16),
            pltpu.SemaphoreType.DMA((7,)),
            pltpu.SemaphoreType.DMA((4, TILES)),
            pltpu.SemaphoreType.DMA((4, TILES)),
            pltpu.SemaphoreType.DMA((2, TILES)),
            pltpu.SemaphoreType.DMA((PLANE,)),
            pltpu.SemaphoreType.DMA((PLANE,)),
            pltpu.SemaphoreType.DMA((2, TILES)),
            pltpu.SemaphoreType.REGULAR,
            pltpu.SemaphoreType.REGULAR,
        ],
        compiler_params=pltpu.CompilerParams(
            collective_id=0, has_side_effects=True, vmem_limit_bytes=60 * 1024 * 1024
        ),
        name="dilated_attention",
    )(short_offsets, middle_offsets, global_offsets, queries, keys, values, w_out)


def solution(mesh):
    placed = (
        P(("wide", "narrow"), None),
        P(("wide", "narrow"), None),
        P(("wide", "narrow"), None),
        P(),
        P(),
        P(),
        P(),
    )
    return jax.shard_map(
        per_device,
        mesh=mesh,
        in_specs=placed,
        out_specs=P(("wide", "narrow"), None),
        check_vma=False,
    )
```

```python
import math

import jax
import jax.numpy as jnp
from jax import lax
from jax.experimental import pallas as pl
from jax.experimental.pallas import tpu as pltpu
from jax.sharding import PartitionSpec as P

MESH = pl.DeviceIdType.MESH
F32 = jnp.float32
BF16 = jnp.bfloat16

LANES = 128
HEAD_DIM = 64
TILES = 12
X_CHIPS, Y_CHIPS, Z_CHIPS = 4, 4, 8
CHIPS = X_CHIPS * Y_CHIPS
PLANE = 2 * CHIPS
FRAMES = 256
SHORT_ROWS, MIDDLE_ROWS, GLOBAL_ROWS = 128, 8, 2
KEPT_ROWS = 512
MIDDLE_PACKET = 32
GLOBAL_PACKET = 16
BLOCK = 8
BLOCKS = PLANE // BLOCK
GLOBAL_SHIFT = 4
FINISH_TILE = 6
PROJECTED = (0, FINISH_TILE, 10, 12)
MASKED = -1e30

SIBLING, ACROSS, PASSED_ON, ALONG_Z = range(4)


def first_head():
    return lax.broadcasted_iota(jnp.int32, (1, LANES), 1) < HEAD_DIM


def attend(query, key, value):
    rows = query.shape[0]
    first = first_head()
    low = first.astype(F32).astype(BF16)
    high = (1.0 - first.astype(F32)).astype(BF16)
    stacked = jnp.concatenate([query * low, query * high], axis=0)
    scores = lax.dot_general(
        stacked, key, (((1,), (1,)), ((), ())), preferred_element_type=F32
    ) * (1.0 / math.sqrt(HEAD_DIM))
    peak = jnp.max(scores, axis=1, keepdims=True)
    exps = jnp.exp(scores - peak)
    total = jnp.sum(exps, axis=1, keepdims=True)
    numerator = jnp.dot(exps.astype(BF16), value, preferred_element_type=F32)
    output = numerator / total
    spread = jnp.broadcast_to(peak + jnp.log(total), (2 * rows, LANES))
    return (
        jnp.where(first, output[:rows], output[rows:]),
        jnp.where(first, spread[:rows], spread[rows:]),
    )


def kernel(
    short_hbm, middle_hbm, global_hbm, q_hbm, k_hbm, v_hbm, w_hbm, o_ref, short_off, middle_off, global_off,
    q_in, k_in, v_in, w_in, plain, short_q, short_kv, short_out, middle_packets, global_packets, middle_in, global_in,
    role_q, gathered, role_out, results, merged, merged_rows, load_sem, send_sem, recv_sem, packet_send, packet_recv,
    result_send, result_recv, row_sem,
):
    wide, narrow = lax.axis_index("wide"), lax.axis_index("narrow")
    x, y, c = narrow // 4, lax.rem(wide, 4), lax.rem(narrow, 2)
    z = lax.rem(narrow // 2, 2) * 4 + wide // 4
    z_hi = z // 4
    chip = x * 4 + y
    me = chip * 2 + c
    early = lax.rem(z // 2, 2) == 0

    def at(plane_place, to_z):
        to_chip = lax.div(plane_place, 2)
        return {
            "wide": lax.rem(to_z, 4) * 4 + lax.rem(to_chip, 4),
            "narrow": lax.div(to_chip, 4) * 4 + lax.div(to_z, 4) * 2 + lax.rem(plane_place, 2),
        }

    sibling = at(chip * 2 + 1 - c, z)

    def along_z(dz):
        return at(me, lax.rem(z + dz, Z_CHIPS))

    def send(source, target, send_to, recv_to, to):
        return pltpu.make_async_remote_copy(
            src_ref=source, dst_ref=target, send_sem=send_to, recv_sem=recv_to,
            device_id=to, device_id_type=MESH,
        )

    def to_sibling(i):
        return send(short_kv.at[i, 0], short_kv.at[i, 1], send_sem.at[SIBLING, i], recv_sem.at[SIBLING, i], sibling)

    def across(i):
        return send(short_kv.at[i, 0], short_kv.at[i, 2], send_sem.at[ACROSS, i], recv_sem.at[ACROSS, i], along_z(4))

    def pass_on(i):
        return send(short_kv.at[i, 2], short_kv.at[i, 3], send_sem.at[PASSED_ON, i], recv_sem.at[PASSED_ON, i], sibling)

    def worker(scope, tile):
        if scope == 0:
            return tile * 2
        return lax.rem(tile + GLOBAL_SHIFT, CHIPS) * 2 + 1

    own_tile = jnp.where(c == 0, chip, lax.rem(chip + CHIPS - GLOBAL_SHIFT, CHIPS))
    works = own_tile < TILES

    def packet_to(scope, tile):
        source, target = ((middle_packets, middle_in), (global_packets, global_in))[scope]
        return send(
            source.at[tile], target.at[me], packet_send.at[scope, tile], packet_recv.at[me], at(worker(scope, tile), z)
        )

    def packet_from(scope, place):
        source, target = ((middle_packets, middle_in), (global_packets, global_in))[scope]
        return send(source.at[0], target.at[place], packet_send.at[scope, 0], packet_recv.at[place], at(place, z))

    def result_to(place):
        return send(
            role_out.at[place], results.at[c, own_tile], result_send.at[place], result_recv.at[c, own_tile], at(place, z)
        )

    def result_from(scope, tile):
        return send(
            role_out.at[0], results.at[scope, tile], result_send.at[0], result_recv.at[scope, tile],
            at(worker(scope, tile), z),
        )

    def middle_across():
        part = gathered.at[pl.ds(z_hi * 4, 4)]
        return send(part, part, send_sem.at[ALONG_Z, 4], recv_sem.at[ALONG_Z, 4], along_z(4))

    def global_to(dz):
        part = gathered.at[z]
        return send(part, part, send_sem.at[ALONG_Z, dz], recv_sem.at[ALONG_Z, dz], along_z(dz))

    loads = [
        pltpu.make_async_copy(source, target, load_sem.at[number])
        for number, (source, target) in enumerate((
            (short_hbm, short_off), (middle_hbm, middle_off), (global_hbm, global_off),
            (k_hbm, k_in), (v_hbm, v_in), (q_hbm, q_in), (w_hbm, w_in),
        ))
    ]
    for load in loads[:5]:
        load.start()

    barrier = pltpu.get_barrier_semaphore()

    def greet(to):
        pl.semaphore_signal(barrier, inc=1, device_id=to, device_id_type=MESH)

    greet(along_z(4))
    column = [
        at((x * 4 + lax.rem(y + dy, Y_CHIPS)) * 2 + lax.rem(c + dc, 2), z)
        for dy in range(Y_CHIPS) for dc in range(2) if dy or dc
    ]
    row = [at((lax.rem(x + dx, X_CHIPS) * 4 + y) * 2 + c, z) for dx in range(1, X_CHIPS)]
    for to in column + row:
        greet(to)

    @pl.when(c == 1)
    def _():
        for dz in (1, 2, 3, 5, 6, 7):
            greet(along_z(dz))

    first = first_head()

    def offsets(ref, i):
        return jnp.where(first, ref[2 * i], ref[2 * i + 1])

    def select_short(source, number, i):
        lanes = pl.ds(pl.multiple_of(i * LANES, LANES), LANES)
        plain[number] = source[:, lanes].astype(F32)
        even = plain[number, pl.ds(0, SHORT_ROWS, stride=2), :]
        odd = plain[number, pl.ds(1, SHORT_ROWS, stride=2), :]
        return jnp.where(offsets(short_off, i) == 0, even, odd).astype(BF16)

    for load in loads[:5]:
        load.wait()
    loads[5].start()

    @pl.loop(0, TILES)
    def _(i):
        short_kv[i, 0, 0] = select_short(k_in, 0, i)
        short_kv[i, 0, 1] = select_short(v_in, 1, i)

    pl.semaphore_wait(barrier, 1 + len(column) + len(row) + 6 * c)

    for to in row:
        pl.semaphore_signal(row_sem, inc=1, device_id=to, device_id_type=MESH)

    @pl.loop(0, jnp.where(early, TILES, 0))
    def _(i):
        across(i).start()

    loads[5].wait()
    loads[6].start()

    @pl.loop(0, TILES)
    def _(i):
        to_sibling(i).start()
        short_q[i] = select_short(q_in, 2, i)

    pl.semaphore_wait(row_sem, len(row))

    @pl.loop(0, TILES)
    def _(step):
        i = lax.rem(step + me, TILES)
        lanes = pl.ds(pl.multiple_of(i * LANES, LANES), LANES)
        middle_at = offsets(middle_off, i)
        global_at = offsets(global_off, i)
        frame = lax.broadcasted_iota(jnp.int32, (FRAMES, LANES), 0)
        in_middle = frame & 31 == middle_at
        in_global = frame & 127 == global_at
        eight = lax.broadcasted_iota(jnp.int32, (8, LANES), 0)
        rows = []
        last = jnp.zeros((8, LANES), F32)
        for number, source in enumerate((q_in, k_in, v_in)):
            values = source[:, lanes].astype(F32)
            rows.append(jnp.sum(jnp.where(in_middle, values, 0.0).reshape(MIDDLE_ROWS, 32, LANES), axis=1))
            global_rows = jnp.sum(jnp.where(in_global, values, 0.0).reshape(GLOBAL_ROWS, 128, LANES), axis=1)
            for row in range(GLOBAL_ROWS):
                last = jnp.where(eight == 2 * number + row, global_rows[row : row + 1], last)
        middle_packets[i] = jnp.concatenate([*rows, jnp.zeros((8, LANES), F32)], axis=0).astype(BF16)
        global_packets[i] = jnp.concatenate([last, jnp.zeros((8, LANES), F32)], axis=0).astype(BF16)

        for scope, (source, target) in enumerate(((middle_packets, middle_in), (global_packets, global_in))):
            @pl.when(worker(scope, i) != me)
            def _():
                packet_to(scope, i).start()

            @pl.when(worker(scope, i) == me)
            def _():
                target[me] = source[i]

    def pick(shape, place):
        row = lax.broadcasted_iota(jnp.int32, shape, 0)
        column = lax.broadcasted_iota(jnp.int32, shape, 1)
        return jnp.where(column == place(row), 1.0, 0.0).astype(BF16)

    def take(one_hot, rows):
        return jnp.dot(one_hot, rows, preferred_element_type=F32).astype(BF16)

    @pl.when(works & (c == 0))
    def _():
        @pl.loop(1, PLANE)
        def _(step):
            packet_from(0, lax.rem(me + step, PLANE)).wait_recv()

        def place(first_row):
            return lambda row: (row >> 3) * MIDDLE_PACKET + first_row + (row & 7)

        picks = [pick((64, BLOCK * MIDDLE_PACKET), place(first_row)) for first_row in (0, 8, 16)]

        @pl.loop(0, BLOCKS)
        def _(block):
            rows = middle_in[pl.ds(block * BLOCK, BLOCK)].reshape(BLOCK * MIDDLE_PACKET, LANES)
            role_q[block] = take(picks[0], rows)
            for part in range(2):
                gathered[z_hi * 4 + block, part] = take(picks[1 + part], rows)

        middle_across().start()

    @pl.when(works & (c == 1))
    def _():
        @pl.loop(1, PLANE)
        def _(step):
            packet_from(1, lax.rem(me + step, PLANE)).wait_recv()

        def place_query(row):
            within = row & 7
            return jnp.where(within < GLOBAL_ROWS, (row >> 3) * GLOBAL_PACKET + within, -1)

        def place(first_row):
            return lambda row: (row >> 1) * GLOBAL_PACKET + first_row + (row & 1)

        rows = global_in[...].reshape(PLANE * GLOBAL_PACKET, LANES)
        for part in range(2):
            gathered[z, part] = take(pick((64, PLANE * GLOBAL_PACKET), place(2 + 2 * part)), rows)
        for dz in range(1, Z_CHIPS):
            global_to(dz).start()
        query_pick = pick((64, BLOCK * GLOBAL_PACKET), place_query)

        @pl.loop(0, BLOCKS)
        def _(block):
            role_q[block] = take(
                query_pick, global_in[pl.ds(block * BLOCK, BLOCK)].reshape(BLOCK * GLOBAL_PACKET, LANES)
            )

    @pl.loop(jnp.where(early, TILES, 0), TILES)
    def _(i):
        across(i).start()

    def wait_along_z():
        @pl.when(works & (c == 0))
        def _():
            middle_across().wait_recv()

        @pl.when(works & (c == 1))
        def _():
            for dz in range(1, Z_CHIPS):
                global_to(dz).wait_recv()

    def work():
        key = gathered[:, 0].reshape(KEPT_ROWS, LANES)
        value = gathered[:, 1].reshape(KEPT_ROWS, LANES)

        @pl.loop(0, BLOCKS)
        def _(block):
            output, spread = attend(role_q[block], key, value)
            places = pl.ds(block * BLOCK, BLOCK)
            role_out[places, 0] = output.reshape(BLOCK, 8, LANES)
            role_out[places, 1] = spread.reshape(BLOCK, 8, LANES)

        @pl.loop(1, PLANE)
        def _(step):
            result_to(lax.rem(me + step, PLANE)).start()

        results[c, own_tile] = role_out[me]

    def short_scope(i):
        to_sibling(i).wait_recv()
        pass_on(i).wait_recv()
        output, spread = attend(
            short_q[i],
            short_kv[i, :, 0].reshape(KEPT_ROWS, LANES),
            short_kv[i, :, 1].reshape(KEPT_ROWS, LANES),
        )
        short_out[i, 0] = output
        short_out[i, 1] = spread

    def finish(i):
        short_at, middle_at, global_at = (offsets(ref, i) for ref in (short_off, middle_off, global_off))
        for parity in range(2):
            shape = (SHORT_ROWS, LANES)
            row = lax.broadcasted_iota(jnp.int32, shape, 0)
            covers = (
                jnp.broadcast_to(short_at == parity, shape),
                2 * (row & 15) + parity == middle_at,
                2 * (row & 63) + parity == global_at,
            )

            def spread_out(value, count):
                return jnp.broadcast_to(
                    value[:count].reshape(count, 1, LANES), (count, SHORT_ROWS // count, LANES)
                ).reshape(shape)

            outs = (
                short_out[i, 0],
                spread_out(results[0, i, 0], MIDDLE_ROWS),
                spread_out(results[1, i, 0], GLOBAL_ROWS),
            )
            spreads = (
                short_out[i, 1],
                spread_out(results[0, i, 1], MIDDLE_ROWS),
                spread_out(results[1, i, 1], GLOBAL_ROWS),
            )
            masked = [jnp.where(cover, value, MASKED) for cover, value in zip(covers, spreads)]
            top = jnp.maximum(jnp.maximum(masked[0], masked[1]), masked[2])
            weights = [jnp.where(cover, jnp.exp(value - top), 0.0) for cover, value in zip(covers, masked)]
            denominator = weights[0] + weights[1] + weights[2]
            denominator = jnp.where(denominator == 0.0, 1.0, denominator)
            total = weights[0] * outs[0] + weights[1] * outs[1] + weights[2] * outs[2]
            merged[pl.ds(parity, SHORT_ROWS, stride=2), :] = total / denominator
        merged_rows[:, pl.ds(pl.multiple_of(i * LANES, LANES), LANES)] = merged[...].astype(BF16)

    def project(first_tile, end_tile):
        depth = pl.ds(first_tile * LANES, (end_tile - first_tile) * LANES)
        for part in range(6):
            columns = pl.ds(part * 256, 256)
            product = jnp.dot(merged_rows[:, depth], w_in[depth, columns], preferred_element_type=F32)
            if first_tile:
                product += o_ref[:, columns]
            o_ref[:, columns] = product

    def wait_results():
        @pl.loop(0, TILES)
        def _(tile):
            for scope in range(2):
                @pl.when(worker(scope, tile) != me)
                def _():
                    result_from(scope, tile).wait_recv()

    def sent(i):
        to_sibling(i).wait_send()
        across(i).wait_send()
        pass_on(i).wait_send()

    def sent_rows():
        @pl.loop(0, TILES)
        def _(i):
            for scope in range(2):
                @pl.when(worker(scope, i) != me)
                def _():
                    packet_to(scope, i).wait_send()

        @pl.when(works)
        def _():
            @pl.loop(1, PLANE)
            def _(step):
                result_to(lax.rem(me + step, PLANE)).wait_send()

            @pl.when(c == 0)
            def _():
                middle_across().wait_send()

            @pl.when(c == 1)
            def _():
                for dz in range(1, Z_CHIPS):
                    global_to(dz).wait_send()

    merge_tile = jnp.where(early, TILES, 0)
    finish_tile = jnp.where(early, TILES, FINISH_TILE)

    @pl.loop(0, TILES + 1)
    def _(i):
        @pl.when(i == merge_tile)
        def _():
            wait_along_z()

        @pl.when((i == merge_tile) & works)
        def _():
            work()

        @pl.when(i == finish_tile)
        def _():
            wait_results()
            loads[6].wait()

        @pl.when(i < TILES)
        def _():
            across(i).wait_recv()
            pass_on(i).start()

        @pl.when(i > 0)
        def _():
            short_scope(i - 1)

        @pl.when(i >= finish_tile)
        def _():
            @pl.loop(jnp.where(i == finish_tile, 0, i - 1), i)
            def _(tile):
                finish(tile)

        for first_tile, end_tile in zip(PROJECTED, PROJECTED[1:]):
            @pl.when((i == end_tile) & ~early)
            def _():
                project(first_tile, end_tile)

        @pl.when((i == TILES) & early)
        def _():
            project(0, TILES)

        @pl.when(i > 1)
        def _():
            sent(i - 2)

        @pl.when(i == jnp.where(early, TILES, 9))
        def _():
            sent_rows()

    sent(TILES - 1)


def per_device(queries, keys, values, short_offsets, middle_offsets, global_offsets, w_out):
    frames, width = queries.shape
    heads = short_offsets.shape
    return pl.pallas_call(
        kernel,
        out_shape=pltpu.VMEM((frames, width), F32),
        in_specs=[pl.BlockSpec(memory_space=pltpu.HBM)] * 7,
        out_specs=pl.BlockSpec(memory_space=pltpu.VMEM),
        scratch_shapes=[
            pltpu.SMEM(heads, jnp.int32),
            pltpu.SMEM(heads, jnp.int32),
            pltpu.SMEM(heads, jnp.int32),
            pltpu.VMEM((frames, width), BF16),
            pltpu.VMEM((frames, width), BF16),
            pltpu.VMEM((frames, width), BF16),
            pltpu.VMEM((width, width), BF16),
            pltpu.VMEM((3, frames, LANES), F32),
            pltpu.VMEM((TILES, SHORT_ROWS, LANES), BF16),
            pltpu.VMEM((TILES, 4, 2, SHORT_ROWS, LANES), BF16),
            pltpu.VMEM((TILES, 2, SHORT_ROWS, LANES), F32),
            pltpu.VMEM((TILES, MIDDLE_PACKET, LANES), BF16),
            pltpu.VMEM((TILES, GLOBAL_PACKET, LANES), BF16),
            pltpu.VMEM((PLANE, MIDDLE_PACKET, LANES), BF16),
            pltpu.VMEM((PLANE, GLOBAL_PACKET, LANES), BF16),
            pltpu.VMEM((BLOCKS, 64, LANES), BF16),
            pltpu.VMEM((8, 2, 64, LANES), BF16),
            pltpu.VMEM((PLANE, 2, 8, LANES), F32),
            pltpu.VMEM((2, TILES, 2, 8, LANES), F32),
            pltpu.VMEM((frames, LANES), F32),
            pltpu.VMEM((frames, width), BF16),
            pltpu.SemaphoreType.DMA((7,)),
            pltpu.SemaphoreType.DMA((4, TILES)),
            pltpu.SemaphoreType.DMA((4, TILES)),
            pltpu.SemaphoreType.DMA((2, TILES)),
            pltpu.SemaphoreType.DMA((PLANE,)),
            pltpu.SemaphoreType.DMA((PLANE,)),
            pltpu.SemaphoreType.DMA((2, TILES)),
            pltpu.SemaphoreType.REGULAR,
        ],
        compiler_params=pltpu.CompilerParams(
            collective_id=0, has_side_effects=True, vmem_limit_bytes=60 * 1024 * 1024
        ),
        name="dilated_attention",
    )(short_offsets, middle_offsets, global_offsets, queries, keys, values, w_out)


def solution(mesh):
    placed = (
        P(("wide", "narrow"), None),
        P(("wide", "narrow"), None),
        P(("wide", "narrow"), None),
        P(),
        P(),
        P(),
        P(),
    )
    return jax.shard_map(
        per_device,
        mesh=mesh,
        in_specs=placed,
        out_specs=P(("wide", "narrow"), None),
        check_vma=False,
    )
```

```python
import math

import jax
import jax.numpy as jnp
from jax import lax
from jax.experimental import pallas as pl
from jax.experimental.pallas import tpu as pltpu
from jax.sharding import PartitionSpec as P

MESH = pl.DeviceIdType.MESH
F32 = jnp.float32
BF16 = jnp.bfloat16

LANES = 128
HEAD_DIM = 64
TILES = 12
X_CHIPS, Y_CHIPS, Z_CHIPS = 4, 4, 8
CHIPS = X_CHIPS * Y_CHIPS
PLANE = 2 * CHIPS
FRAMES = 256
SHORT_ROWS, MIDDLE_ROWS, GLOBAL_ROWS = 128, 8, 2
KEPT_ROWS = 512
MIDDLE_PACKET = 32
GLOBAL_PACKET = 16
BLOCK = 8
BLOCKS = PLANE // BLOCK
GLOBAL_SHIFT = 4
FINISH_TILE = 6
PROJECTED = (0, FINISH_TILE, 10, 12)
MASKED = -1e30

SIBLING, ACROSS, PASSED_ON, ALONG_Z = range(4)


def first_head():
    return lax.broadcasted_iota(jnp.int32, (1, LANES), 1) < HEAD_DIM


def attend(query, key, value):
    rows = query.shape[0]
    first = first_head()
    low = first.astype(F32).astype(BF16)
    high = (1.0 - first.astype(F32)).astype(BF16)
    stacked = jnp.concatenate([query * low, query * high], axis=0)
    scores = lax.dot_general(
        stacked, key, (((1,), (1,)), ((), ())), preferred_element_type=F32
    ) * (1.0 / math.sqrt(HEAD_DIM))
    peak = jnp.max(scores, axis=1, keepdims=True)
    exps = jnp.exp(scores - peak)
    total = jnp.sum(exps, axis=1, keepdims=True)
    numerator = jnp.dot(exps.astype(BF16), value, preferred_element_type=F32)
    output = numerator / total
    spread = jnp.broadcast_to(peak + jnp.log(total), (2 * rows, LANES))
    return (
        jnp.where(first, output[:rows], output[rows:]),
        jnp.where(first, spread[:rows], spread[rows:]),
    )


def kernel(
    short_hbm, middle_hbm, global_hbm, q_hbm, k_hbm, v_hbm, w_hbm, o_ref, short_off, middle_off, global_off,
    q_in, k_in, v_in, w_in, plain, short_q, short_kv, short_out, middle_packets, global_packets, middle_in, global_in,
    role_q, gathered, role_out, results, merged, merged_rows, load_sem, send_sem, recv_sem, packet_send, packet_recv,
    result_send, result_recv, row_sem,
):
    wide, narrow = lax.axis_index("wide"), lax.axis_index("narrow")
    x, y, c = narrow // 4, lax.rem(wide, 4), lax.rem(narrow, 2)
    z = lax.rem(narrow // 2, 2) * 4 + wide // 4
    z_hi = z // 4
    chip = x * 4 + y
    me = chip * 2 + c
    early = lax.rem(z // 2, 2) == 0

    def at(plane_place, to_z):
        to_chip = lax.div(plane_place, 2)
        return {
            "wide": lax.rem(to_z, 4) * 4 + lax.rem(to_chip, 4),
            "narrow": lax.div(to_chip, 4) * 4 + lax.div(to_z, 4) * 2 + lax.rem(plane_place, 2),
        }

    sibling = at(chip * 2 + 1 - c, z)

    def along_z(dz):
        return at(me, lax.rem(z + dz, Z_CHIPS))

    def send(source, target, send_to, recv_to, to):
        return pltpu.make_async_remote_copy(
            src_ref=source, dst_ref=target, send_sem=send_to, recv_sem=recv_to,
            device_id=to, device_id_type=MESH,
        )

    def to_sibling(i):
        return send(short_kv.at[i, 0], short_kv.at[i, 1], send_sem.at[SIBLING, i], recv_sem.at[SIBLING, i], sibling)

    def across(i):
        return send(short_kv.at[i, 0], short_kv.at[i, 2], send_sem.at[ACROSS, i], recv_sem.at[ACROSS, i], along_z(4))

    def pass_on(i):
        return send(short_kv.at[i, 2], short_kv.at[i, 3], send_sem.at[PASSED_ON, i], recv_sem.at[PASSED_ON, i], sibling)

    def worker(scope, tile):
        if scope == 0:
            return tile * 2
        return lax.rem(tile + GLOBAL_SHIFT, CHIPS) * 2 + 1

    own_tile = jnp.where(c == 0, chip, lax.rem(chip + CHIPS - GLOBAL_SHIFT, CHIPS))
    works = own_tile < TILES

    def packet_to(scope, tile):
        source, target = ((middle_packets, middle_in), (global_packets, global_in))[scope]
        return send(
            source.at[tile], target.at[me], packet_send.at[scope, tile], packet_recv.at[me], at(worker(scope, tile), z)
        )

    def packet_from(scope, place):
        source, target = ((middle_packets, middle_in), (global_packets, global_in))[scope]
        return send(source.at[0], target.at[place], packet_send.at[scope, 0], packet_recv.at[place], at(place, z))

    def result_to(place):
        return send(
            role_out.at[place], results.at[c, own_tile], result_send.at[place], result_recv.at[c, own_tile], at(place, z)
        )

    def result_from(scope, tile):
        return send(
            role_out.at[0], results.at[scope, tile], result_send.at[0], result_recv.at[scope, tile],
            at(worker(scope, tile), z),
        )

    def middle_across():
        part = gathered.at[pl.ds(z_hi * 4, 4)]
        return send(part, part, send_sem.at[ALONG_Z, 4], recv_sem.at[ALONG_Z, 4], along_z(4))

    def global_to(dz):
        part = gathered.at[z]
        return send(part, part, send_sem.at[ALONG_Z, dz], recv_sem.at[ALONG_Z, dz], along_z(dz))

    barrier = pltpu.get_barrier_semaphore()

    def greet(to):
        pl.semaphore_signal(barrier, inc=1, device_id=to, device_id_type=MESH)

    greet(along_z(4))
    loads = [
        pltpu.make_async_copy(source, target, load_sem.at[number])
        for number, (source, target) in enumerate((
            (short_hbm, short_off), (middle_hbm, middle_off), (global_hbm, global_off),
            (k_hbm, k_in), (v_hbm, v_in), (q_hbm, q_in), (w_hbm, w_in),
        ))
    ]
    for load in loads[:5]:
        load.start()


    column = [
        at((x * 4 + lax.rem(y + dy, Y_CHIPS)) * 2 + lax.rem(c + dc, 2), z)
        for dy in range(Y_CHIPS) for dc in range(2) if dy or dc
    ]
    row = [at((lax.rem(x + dx, X_CHIPS) * 4 + y) * 2 + c, z) for dx in range(1, X_CHIPS)]
    for to in column + row:
        greet(to)

    @pl.when(c == 1)
    def _():
        for dz in (1, 2, 3, 5, 6, 7):
            greet(along_z(dz))

    first = first_head()

    def offsets(ref, i):
        return jnp.where(first, ref[2 * i], ref[2 * i + 1])

    def select_short(source, number, i):
        lanes = pl.ds(pl.multiple_of(i * LANES, LANES), LANES)
        plain[number] = source[:, lanes].astype(F32)
        even = plain[number, pl.ds(0, SHORT_ROWS, stride=2), :]
        odd = plain[number, pl.ds(1, SHORT_ROWS, stride=2), :]
        return jnp.where(offsets(short_off, i) == 0, even, odd).astype(BF16)

    for load in loads[:5]:
        load.wait()
    loads[5].start()

    @pl.loop(0, TILES)
    def _(i):
        short_kv[i, 0, 0] = select_short(k_in, 0, i)
        short_kv[i, 0, 1] = select_short(v_in, 1, i)

    pl.semaphore_wait(barrier, 1 + len(column) + len(row) + 6 * c)

    for to in row:
        pl.semaphore_signal(row_sem, inc=1, device_id=to, device_id_type=MESH)

    @pl.loop(0, jnp.where(early, TILES, 0))
    def _(i):
        across(i).start()

    loads[5].wait()
    loads[6].start()

    @pl.loop(0, TILES)
    def _(i):
        to_sibling(i).start()
        short_q[i] = select_short(q_in, 2, i)

    pl.semaphore_wait(row_sem, len(row))

    @pl.loop(0, TILES)
    def _(step):
        i = lax.rem(step + me, TILES)
        lanes = pl.ds(pl.multiple_of(i * LANES, LANES), LANES)
        middle_at = offsets(middle_off, i)
        global_at = offsets(global_off, i)
        frame = lax.broadcasted_iota(jnp.int32, (FRAMES, LANES), 0)
        in_middle = frame & 31 == middle_at
        in_global = frame & 127 == global_at
        eight = lax.broadcasted_iota(jnp.int32, (8, LANES), 0)
        rows = []
        last = jnp.zeros((8, LANES), F32)
        for number, source in enumerate((q_in, k_in, v_in)):
            values = source[:, lanes].astype(F32)
            rows.append(jnp.sum(jnp.where(in_middle, values, 0.0).reshape(MIDDLE_ROWS, 32, LANES), axis=1))
            global_rows = jnp.sum(jnp.where(in_global, values, 0.0).reshape(GLOBAL_ROWS, 128, LANES), axis=1)
            for row in range(GLOBAL_ROWS):
                last = jnp.where(eight == 2 * number + row, global_rows[row : row + 1], last)
        middle_packets[i] = jnp.concatenate([*rows, jnp.zeros((8, LANES), F32)], axis=0).astype(BF16)
        global_packets[i] = jnp.concatenate([last, jnp.zeros((8, LANES), F32)], axis=0).astype(BF16)

        for scope, (source, target) in enumerate(((middle_packets, middle_in), (global_packets, global_in))):
            @pl.when(worker(scope, i) != me)
            def _():
                packet_to(scope, i).start()

            @pl.when(worker(scope, i) == me)
            def _():
                target[me] = source[i]

    def pick(shape, place):
        row = lax.broadcasted_iota(jnp.int32, shape, 0)
        column = lax.broadcasted_iota(jnp.int32, shape, 1)
        return jnp.where(column == place(row), 1.0, 0.0).astype(BF16)

    def take(one_hot, rows):
        return jnp.dot(one_hot, rows, preferred_element_type=F32).astype(BF16)

    @pl.when(works & (c == 0))
    def _():
        @pl.loop(1, PLANE)
        def _(step):
            packet_from(0, lax.rem(me + step, PLANE)).wait_recv()

        def place(first_row):
            return lambda row: (row >> 3) * MIDDLE_PACKET + first_row + (row & 7)

        picks = [pick((64, BLOCK * MIDDLE_PACKET), place(first_row)) for first_row in (0, 8, 16)]

        @pl.loop(0, BLOCKS)
        def _(block):
            rows = middle_in[pl.ds(block * BLOCK, BLOCK)].reshape(BLOCK * MIDDLE_PACKET, LANES)
            role_q[block] = take(picks[0], rows)
            for part in range(2):
                gathered[z_hi * 4 + block, part] = take(picks[1 + part], rows)

        middle_across().start()

    @pl.when(works & (c == 1))
    def _():
        @pl.loop(1, PLANE)
        def _(step):
            packet_from(1, lax.rem(me + step, PLANE)).wait_recv()

        def place_query(row):
            within = row & 7
            return jnp.where(within < GLOBAL_ROWS, (row >> 3) * GLOBAL_PACKET + within, -1)

        def place(first_row):
            return lambda row: (row >> 1) * GLOBAL_PACKET + first_row + (row & 1)

        rows = global_in[...].reshape(PLANE * GLOBAL_PACKET, LANES)
        for part in range(2):
            gathered[z, part] = take(pick((64, PLANE * GLOBAL_PACKET), place(2 + 2 * part)), rows)
        for dz in range(1, Z_CHIPS):
            global_to(dz).start()
        query_pick = pick((64, BLOCK * GLOBAL_PACKET), place_query)

        @pl.loop(0, BLOCKS)
        def _(block):
            role_q[block] = take(
                query_pick, global_in[pl.ds(block * BLOCK, BLOCK)].reshape(BLOCK * GLOBAL_PACKET, LANES)
            )

    @pl.loop(jnp.where(early, TILES, 0), TILES)
    def _(i):
        across(i).start()

    def wait_along_z():
        @pl.when(works & (c == 0))
        def _():
            middle_across().wait_recv()

        @pl.when(works & (c == 1))
        def _():
            for dz in range(1, Z_CHIPS):
                global_to(dz).wait_recv()

    def work():
        key = gathered[:, 0].reshape(KEPT_ROWS, LANES)
        value = gathered[:, 1].reshape(KEPT_ROWS, LANES)

        @pl.loop(0, BLOCKS)
        def _(block):
            output, spread = attend(role_q[block], key, value)
            places = pl.ds(block * BLOCK, BLOCK)
            role_out[places, 0] = output.reshape(BLOCK, 8, LANES)
            role_out[places, 1] = spread.reshape(BLOCK, 8, LANES)

        @pl.loop(1, PLANE)
        def _(step):
            result_to(lax.rem(me + step, PLANE)).start()

        results[c, own_tile] = role_out[me]

    def short_scope(i):
        to_sibling(i).wait_recv()
        pass_on(i).wait_recv()
        output, spread = attend(
            short_q[i],
            short_kv[i, :, 0].reshape(KEPT_ROWS, LANES),
            short_kv[i, :, 1].reshape(KEPT_ROWS, LANES),
        )
        short_out[i, 0] = output
        short_out[i, 1] = spread

    def finish(i):
        short_at, middle_at, global_at = (offsets(ref, i) for ref in (short_off, middle_off, global_off))
        for parity in range(2):
            shape = (SHORT_ROWS, LANES)
            row = lax.broadcasted_iota(jnp.int32, shape, 0)
            covers = (
                jnp.broadcast_to(short_at == parity, shape),
                2 * (row & 15) + parity == middle_at,
                2 * (row & 63) + parity == global_at,
            )

            def spread_out(value, count):
                return jnp.broadcast_to(
                    value[:count].reshape(count, 1, LANES), (count, SHORT_ROWS // count, LANES)
                ).reshape(shape)

            outs = (
                short_out[i, 0],
                spread_out(results[0, i, 0], MIDDLE_ROWS),
                spread_out(results[1, i, 0], GLOBAL_ROWS),
            )
            spreads = (
                short_out[i, 1],
                spread_out(results[0, i, 1], MIDDLE_ROWS),
                spread_out(results[1, i, 1], GLOBAL_ROWS),
            )
            masked = [jnp.where(cover, value, MASKED) for cover, value in zip(covers, spreads)]
            top = jnp.maximum(jnp.maximum(masked[0], masked[1]), masked[2])
            weights = [jnp.where(cover, jnp.exp(value - top), 0.0) for cover, value in zip(covers, masked)]
            denominator = weights[0] + weights[1] + weights[2]
            denominator = jnp.where(denominator == 0.0, 1.0, denominator)
            total = weights[0] * outs[0] + weights[1] * outs[1] + weights[2] * outs[2]
            merged[pl.ds(parity, SHORT_ROWS, stride=2), :] = total / denominator
        merged_rows[:, pl.ds(pl.multiple_of(i * LANES, LANES), LANES)] = merged[...].astype(BF16)

    def project(first_tile, end_tile):
        depth = pl.ds(first_tile * LANES, (end_tile - first_tile) * LANES)
        for part in range(6):
            columns = pl.ds(part * 256, 256)
            product = jnp.dot(merged_rows[:, depth], w_in[depth, columns], preferred_element_type=F32)
            if first_tile:
                product += o_ref[:, columns]
            o_ref[:, columns] = product

    def wait_results():
        @pl.loop(0, TILES)
        def _(tile):
            for scope in range(2):
                @pl.when(worker(scope, tile) != me)
                def _():
                    result_from(scope, tile).wait_recv()

    def sent(i):
        to_sibling(i).wait_send()
        across(i).wait_send()
        pass_on(i).wait_send()

    def sent_rows():
        @pl.loop(0, TILES)
        def _(i):
            for scope in range(2):
                @pl.when(worker(scope, i) != me)
                def _():
                    packet_to(scope, i).wait_send()

        @pl.when(works)
        def _():
            @pl.loop(1, PLANE)
            def _(step):
                result_to(lax.rem(me + step, PLANE)).wait_send()

            @pl.when(c == 0)
            def _():
                middle_across().wait_send()

            @pl.when(c == 1)
            def _():
                for dz in range(1, Z_CHIPS):
                    global_to(dz).wait_send()

    merge_tile = jnp.where(early, TILES, 0)
    finish_tile = jnp.where(early, TILES, FINISH_TILE)

    @pl.loop(0, TILES + 1)
    def _(i):
        @pl.when(i == merge_tile)
        def _():
            wait_along_z()

        @pl.when((i == merge_tile) & works)
        def _():
            work()

        @pl.when(i == finish_tile)
        def _():
            wait_results()
            loads[6].wait()

        @pl.when(i < TILES)
        def _():
            across(i).wait_recv()
            pass_on(i).start()

        @pl.when(i > 0)
        def _():
            short_scope(i - 1)

        @pl.when(i >= finish_tile)
        def _():
            @pl.loop(jnp.where(i == finish_tile, 0, i - 1), i)
            def _(tile):
                finish(tile)

        for first_tile, end_tile in zip(PROJECTED, PROJECTED[1:]):
            @pl.when((i == end_tile) & ~early)
            def _():
                project(first_tile, end_tile)

        @pl.when((i == TILES) & early)
        def _():
            project(0, TILES)

        @pl.when(i > 1)
        def _():
            sent(i - 2)

        @pl.when(i == jnp.where(early, TILES, 9))
        def _():
            sent_rows()

    sent(TILES - 1)


def per_device(queries, keys, values, short_offsets, middle_offsets, global_offsets, w_out):
    frames, width = queries.shape
    heads = short_offsets.shape
    return pl.pallas_call(
        kernel,
        out_shape=pltpu.VMEM((frames, width), F32),
        in_specs=[pl.BlockSpec(memory_space=pltpu.HBM)] * 7,
        out_specs=pl.BlockSpec(memory_space=pltpu.VMEM),
        scratch_shapes=[
            pltpu.SMEM(heads, jnp.int32),
            pltpu.SMEM(heads, jnp.int32),
            pltpu.SMEM(heads, jnp.int32),
            pltpu.VMEM((frames, width), BF16),
            pltpu.VMEM((frames, width), BF16),
            pltpu.VMEM((frames, width), BF16),
            pltpu.VMEM((width, width), BF16),
            pltpu.VMEM((3, frames, LANES), F32),
            pltpu.VMEM((TILES, SHORT_ROWS, LANES), BF16),
            pltpu.VMEM((TILES, 4, 2, SHORT_ROWS, LANES), BF16),
            pltpu.VMEM((TILES, 2, SHORT_ROWS, LANES), F32),
            pltpu.VMEM((TILES, MIDDLE_PACKET, LANES), BF16),
            pltpu.VMEM((TILES, GLOBAL_PACKET, LANES), BF16),
            pltpu.VMEM((PLANE, MIDDLE_PACKET, LANES), BF16),
            pltpu.VMEM((PLANE, GLOBAL_PACKET, LANES), BF16),
            pltpu.VMEM((BLOCKS, 64, LANES), BF16),
            pltpu.VMEM((8, 2, 64, LANES), BF16),
            pltpu.VMEM((PLANE, 2, 8, LANES), F32),
            pltpu.VMEM((2, TILES, 2, 8, LANES), F32),
            pltpu.VMEM((frames, LANES), F32),
            pltpu.VMEM((frames, width), BF16),
            pltpu.SemaphoreType.DMA((7,)),
            pltpu.SemaphoreType.DMA((4, TILES)),
            pltpu.SemaphoreType.DMA((4, TILES)),
            pltpu.SemaphoreType.DMA((2, TILES)),
            pltpu.SemaphoreType.DMA((PLANE,)),
            pltpu.SemaphoreType.DMA((PLANE,)),
            pltpu.SemaphoreType.DMA((2, TILES)),
            pltpu.SemaphoreType.REGULAR,
        ],
        compiler_params=pltpu.CompilerParams(
            collective_id=0, has_side_effects=True, vmem_limit_bytes=60 * 1024 * 1024
        ),
        name="dilated_attention",
    )(short_offsets, middle_offsets, global_offsets, queries, keys, values, w_out)


def solution(mesh):
    placed = (
        P(("wide", "narrow"), None),
        P(("wide", "narrow"), None),
        P(("wide", "narrow"), None),
        P(),
        P(),
        P(),
        P(),
    )
    return jax.shard_map(
        per_device,
        mesh=mesh,
        in_specs=placed,
        out_specs=P(("wide", "narrow"), None),
        check_vma=False,
    )
```
